256 devices in a mesh: text: 16 (over y_hi, x, core), image: 16 (over y_lo, z).
Axes of the slice: x: 4, y: 4 (y_hi: 2, y_lo: 2; y = y_hi * 2 + y_lo), z: 8, core: 2. Of those that a mesh axis runs over, the one named last changes fastest.
Arguments:
- queries: bfloat16 [2048, 4096], P('text'), may hold values from -24 to 24
- keys: bfloat16 [10240, 512], P('image'), may hold values from -24 to 24
- values: bfloat16 [10240, 512], P('image'), may hold values from -6 to 6
- grad_out: bfloat16 [2048, 4096], P('text'), may hold values from -600 to 600
- keep_blocks: int32 [32, 80], P('text', 'image'), may hold values from 0 to 1, as said below
Outputs:
- grad_queries: bfloat16 [2048, 4096], P('text', 'image')
- grad_keys: bfloat16 [10240, 512], P(('image', 'text'))
- grad_values: bfloat16 [10240, 512], P(('image', 'text'))
The draws below stay inside these ranges and needn't reach their ends.
Inputs may be any that keep to these rules, and one draw needn't show every extreme that they name: `keep_blocks`: the last frame block is kept for every text block.
All inputs are finite; a program needn't handle non-finite values.
Results may differ from the reference program's by a relative error of at most 0.0059.
Values sent between devices are 32-bit elements; how exact they have to be, the bound alone decides.
No kernel may reach another device: no remote copies, remote signals or barrier semaphores. Data moves between devices by JAX's collectives and lax.ppermute only.
A program may use at most 128 MiB of HBM per device.

```python
import jax
import jax.numpy as jnp
from jax import lax

HQ = 32
HK = 4
HD = 128
TBLK = 64
FBLK = 128
TEXT = 2048
IMG = 10240


def draw_queries(key, part):
    key = jax.random.fold_in(key, 11)
    base = jnp.clip(jax.random.normal(key, (TEXT, HQ, HD), jnp.float32), -4.0, 4.0)
    return base.reshape(TEXT, HQ * HD).astype(jnp.bfloat16)


def draw_keys(key, part):
    key = jax.random.fold_in(key, 23)
    base = jnp.clip(jax.random.normal(key, (IMG, HK, HD), jnp.float32), -4.0, 4.0)
    return base.reshape(IMG, HK * HD).astype(jnp.bfloat16)


def draw_keep_blocks(key, part):
    key = jax.random.fold_in(key, 37)
    block_rows = TEXT // TBLK
    block_cols = IMG // FBLK
    rolls = jax.random.randint(key, (block_rows, block_cols), 0, 100)
    limit = 20 + 70 * jnp.arange(block_cols) // block_cols
    kept = (rolls < limit[None, :]).astype(jnp.int32)
    kept = kept.at[:, block_cols - 1].set(1)
    return kept


def levels(stream_key, shape, cuts, least, largest):
    def one(dim, shards_of):
        heights = jax.random.uniform(jax.random.fold_in(jax.random.fold_in(stream_key, 6), dim), (shards_of,), jnp.float32, least / len(cuts), largest / len(cuts))
        return jnp.repeat(jnp.exp(heights), shape[dim] // shards_of).reshape((-1,) + (1,) * (len(shape) - dim - 1))

    loudness = one(*cuts[0])
    for cut in cuts[1:]:
        loudness = loudness * one(*cut)
    return loudness


def noise(stream_key, extent, scale, most, pieces=(), kind=jnp.bfloat16):
    level = levels(stream_key, extent, pieces, -0.22, 0.18) if pieces else 1.0
    entries = jax.random.normal(stream_key, extent, jnp.float32) * scale * level
    return jnp.minimum(jnp.maximum(entries, -most), most).astype(kind)


def setup_inputs(seed: int = 0) -> dict:
    arg_keys = jax.random.split(jax.random.key(seed), 6)
    queries = draw_queries(jax.random.fold_in(arg_keys[5], 71), 0)
    keys = draw_keys(jax.random.fold_in(arg_keys[5], 71), 0)
    values = noise(arg_keys[2], (IMG, HK * HD), 1.0, 6.0, ((0, 16),))
    grad_out = noise(arg_keys[3], (TEXT, HQ * HD), 100.0, 600.0, ((0, 16),))
    keep_blocks = draw_keep_blocks(jax.random.fold_in(arg_keys[5], 71), 0)
    return {"queries": queries, "keys": keys, "values": values, "grad_out": grad_out, "keep_blocks": keep_blocks}


floor_score = -1.0e30


def reference(queries, keys, values, grad_out, keep_blocks):
    per_group = HQ // HK
    score_scale = HD ** -0.5
    kept_mask = jnp.repeat(jnp.repeat(keep_blocks, TBLK, axis=0), FBLK, axis=1) > 0
    query_heads = queries.reshape(TEXT, HQ, HD).transpose(1, 0, 2)
    grad_heads = grad_out.reshape(TEXT, HQ, HD).transpose(1, 0, 2)
    key_heads = keys.reshape(IMG, HK, HD).transpose(1, 0, 2)
    value_heads = values.reshape(IMG, HK, HD).transpose(1, 0, 2)

    def one_head(head):
        query_rows = query_heads[head]
        grad_rows = grad_heads[head]
        key_group = key_heads[head // per_group]
        value_group = value_heads[head // per_group]
        scores = jnp.dot(query_rows, key_group.T, preferred_element_type=jnp.float32) * score_scale
        scores = jnp.where(kept_mask, scores, floor_score)
        row_max = jnp.max(scores, axis=1, keepdims=True)
        weights = jnp.where(kept_mask, jnp.exp(scores - row_max), 0.0)
        probs = weights / jnp.sum(weights, axis=1, keepdims=True)
        grad_probs = jnp.dot(grad_rows, value_group.T, preferred_element_type=jnp.float32)
        delta = jnp.sum(probs * grad_probs, axis=1, keepdims=True)
        grad_scores = (probs * (grad_probs - delta)).astype(jnp.bfloat16)
        probs_low = probs.astype(jnp.bfloat16)
        grad_query = jnp.dot(grad_scores, key_group, preferred_element_type=jnp.float32) * score_scale
        grad_key = jnp.dot(grad_scores.T, query_rows, preferred_element_type=jnp.float32) * score_scale
        grad_value = jnp.dot(probs_low.T, grad_rows, preferred_element_type=jnp.float32)
        return grad_query, grad_key, grad_value

    grad_query, grad_key, grad_value = lax.map(one_head, jnp.arange(HQ))
    grad_queries = grad_query.transpose(1, 0, 2).reshape(TEXT, HQ * HD).astype(jnp.bfloat16)
    grad_keys = grad_key.reshape(HK, per_group, IMG, HD).sum(axis=1)
    grad_keys = grad_keys.transpose(1, 0, 2).reshape(IMG, HK * HD).astype(jnp.bfloat16)
    grad_values = grad_value.reshape(HK, per_group, IMG, HD).sum(axis=1)
    grad_values = grad_values.transpose(1, 0, 2).reshape(IMG, HK * HD).astype(jnp.bfloat16)
    return (grad_queries, grad_keys, grad_values)
```

```python
import jax
import jax.numpy as jnp
from jax import lax
from jax.experimental import pallas as pl
from jax.experimental.pallas import tpu as pltpu
from jax.sharding import PartitionSpec as P

HD = 128
TBLK = 64
FBLK = 128
SCALE = HD ** (-0.5)
EXP2_SCALE = SCALE * 1.4426950408889634
MASKED = -1e30
NO_KEY = -1e29
LIMIT = 56 * 1024 * 1024

F32 = jnp.float32
BF16 = jnp.bfloat16


def head(array, index):
    return array[:, index * HD : (index + 1) * HD]


def row_fold(block, combine):
    parts = [block[8 * i : 8 * i + 8] for i in range(block.shape[0] // 8)]
    while len(parts) > 1:
        parts = [combine(parts[i], parts[i + 1]) for i in range(0, len(parts) - 1, 2)] + (
            [parts[-1]] if len(parts) % 2 else []
        )
    return parts[0]


def local_kernel(
    keep_ref, q_ref, do_ref, k_ref, v_ref,
    e_ref, es_ref, at_ref, bt_ref, stat_ref, max_ref,
    s_scr, g_scr,
):
    group = pl.program_id(0)
    heads = q_ref.shape[1] // HD
    rows = q_ref.shape[0]
    blocks = k_ref.shape[0] // FBLK
    copies, stat_rows = stat_ref.shape[0], stat_ref.shape[1] // 2
    first_half = lax.broadcasted_iota(jnp.int32, (1, rows), 1) < TBLK
    bias = [
        jnp.where(
            first_half,
            jnp.where(keep_ref[0, b] > 0, 0.0, MASKED),
            jnp.where(keep_ref[1, b] > 0, 0.0, MASKED),
        ).astype(F32)
        for b in range(blocks)
    ]
    keys = k_ref[...]
    values = v_ref[...]
    maxima, logs, deltas = [], [], []
    for pair in range(heads // 2):
        two = (2 * pair, 2 * pair + 1)
        columns = slice(2 * pair * rows, (2 * pair + 2) * rows)
        q_two = jnp.concatenate([head(q_ref, h) for h in two], axis=0)
        do_two = jnp.concatenate([head(do_ref, h) for h in two], axis=0)
        contract_last = (((1,), (1,)), ((), ()))
        s_scr[:, columns] = lax.dot_general(keys, q_two, contract_last, preferred_element_type=F32)
        g_scr[:, columns] = lax.dot_general(values, do_two, contract_last, preferred_element_type=F32)
        for h in two:
            lanes = slice(h * rows, (h + 1) * rows)
            top = None
            for b in range(blocks):
                block_rows = slice(b * FBLK, (b + 1) * FBLK)
                part = row_fold(s_scr[block_rows, lanes], jnp.maximum) + bias[b]
                top = part if top is None else jnp.maximum(top, part)
            row_max = jnp.maximum(jnp.max(top, axis=0, keepdims=True), NO_KEY)
            total = jnp.zeros((8, rows), F32)
            product = jnp.zeros((8, rows), F32)
            for b in range(blocks):
                block_rows = slice(b * FBLK, (b + 1) * FBLK)
                weight = jnp.exp2((s_scr[block_rows, lanes] + (bias[b] - row_max)) * EXP2_SCALE)
                s_scr[block_rows, lanes] = weight
                total = total + row_fold(weight, jnp.add)
                product = product + row_fold(weight * g_scr[block_rows, lanes], jnp.add)
            total = jnp.sum(total, axis=0, keepdims=True)
            product = jnp.sum(product, axis=0, keepdims=True)
            some = total > 0.0
            safe = jnp.where(some, total, 1.0)
            delta = product / safe
            for b in range(blocks):
                block_rows = slice(b * FBLK, (b + 1) * FBLK)
                weight = s_scr[block_rows, lanes]
                e_ref[block_rows, lanes] = weight.astype(BF16)
                es_ref[block_rows, lanes] = (weight * (g_scr[block_rows, lanes] - delta)).astype(BF16)
            scaled_max = row_max * SCALE
            maxima.append(scaled_max)
            logs.append(jnp.where(some, scaled_max + jnp.log(safe), MASKED))
            deltas.append(delta)
        contract_first = (((0,), (0,)), ((), ()))
        at_ref[:, columns] = lax.dot_general(
            keys, es_ref[:, columns], contract_first, preferred_element_type=F32
        )
        bt_ref[:, columns] = lax.dot_general(
            keys, e_ref[:, columns], contract_first, preferred_element_type=F32
        )
    log_rows = jnp.concatenate(logs, axis=0)
    delta_rows = jnp.concatenate(deltas, axis=0)
    at = pl.multiple_of(group * heads, 8)
    for copy in range(copies):
        stat_ref[copy, pl.ds(at, heads), :] = log_rows
        stat_ref[copy, pl.ds(at + stat_rows, heads), :] = delta_rows
    max_ref[pl.ds(at, heads), :] = jnp.concatenate(maxima, axis=0)


def local_part(keep_blocks, queries, grad_out, keys, values, copies):
    rows, width = queries.shape
    image_rows, key_width = keys.shape
    groups = key_width // HD
    per_group = width // groups
    heads = width // HD
    wide = groups * (per_group // HD) * rows
    wide_block = wide // groups
    flops = 8 * heads * rows * image_rows * HD
    return pl.pallas_call(
        local_kernel,
        grid=(groups,),
        in_specs=[
            pl.BlockSpec(memory_space=pltpu.SMEM),
            pl.BlockSpec((rows, per_group), lambda g: (0, g)),
            pl.BlockSpec((rows, per_group), lambda g: (0, g)),
            pl.BlockSpec((image_rows, HD), lambda g: (0, g)),
            pl.BlockSpec((image_rows, HD), lambda g: (0, g)),
        ],
        out_specs=[
            pl.BlockSpec((image_rows, wide_block), lambda g: (0, g)),
            pl.BlockSpec((image_rows, wide_block), lambda g: (0, g)),
            pl.BlockSpec((HD, wide_block), lambda g: (0, g)),
            pl.BlockSpec((HD, wide_block), lambda g: (0, g)),
            pl.BlockSpec((copies, 2 * heads, rows), lambda g: (0, 0, 0)),
            pl.BlockSpec((heads, rows), lambda g: (0, 0)),
        ],
        out_shape=[
            jax.ShapeDtypeStruct((image_rows, wide), BF16),
            jax.ShapeDtypeStruct((image_rows, wide), BF16),
            jax.ShapeDtypeStruct((HD, wide), F32),
            jax.ShapeDtypeStruct((HD, wide), F32),
            jax.ShapeDtypeStruct((copies, 2 * heads, rows), F32),
            jax.ShapeDtypeStruct((heads, rows), F32),
        ],
        scratch_shapes=[
            pltpu.VMEM((image_rows, wide_block), F32),
            pltpu.VMEM((image_rows, wide_block), F32),
        ],
        compiler_params=pltpu.CompilerParams(vmem_limit_bytes=LIMIT),
        cost_estimate=pl.CostEstimate(
            flops=flops, bytes_accessed=18 * 2**20, transcendentals=heads * rows * image_rows
        ),
        name="local_products",
    )(keep_blocks, queries, grad_out, keys, values)


def query_kernel(all_ref, own_ref, max_ref, at_ref, bt_ref, out_ref, factor_ref, w_scr, d_scr):
    group = pl.program_id(0)
    sources, double, rows = all_ref.shape
    heads = double // 2

    @pl.when(group == 0)
    def _():
        logs = [all_ref[s, 0:heads, :] for s in range(sources)]
        top = logs[0]
        for log in logs[1:]:
            top = jnp.maximum(top, log)
        total = jnp.zeros((heads, rows), F32)
        product = jnp.zeros((heads, rows), F32)
        for s in range(sources):
            share = jnp.exp(logs[s] - top)
            total = total + share
            product = product + share * all_ref[s, heads:double, :]
        w = jnp.exp(max_ref[...] - (top + jnp.log(total)))
        w_scr[...] = w
        d_scr[...] = w * (own_ref[0, heads:double, :] - product / total)

    per_group = at_ref.shape[1] // rows
    at = pl.ds(pl.multiple_of(group * per_group, 8), per_group)
    w_rows = w_scr[at, :]
    d_rows = d_scr[at, :]
    fill = jnp.zeros((rows - 2 * per_group, rows), F32)
    factor_ref[0] = jnp.transpose(jnp.concatenate([w_rows, d_rows, fill], axis=0))
    for h in range(per_group):
        lanes = slice(h * rows, (h + 1) * rows)
        term = (w_rows[h : h + 1] * at_ref[:, lanes] + d_rows[h : h + 1] * bt_ref[:, lanes]) * SCALE
        out_ref[h // 2, 0, :, (h % 2) * HD : (h % 2 + 1) * HD] = jnp.transpose(term)


def query_part(stats, own, maxima, at, bt, z_size, y_size):
    sources, double, rows = stats.shape
    wide = at.shape[1]
    heads = wide // rows
    per_group = 8
    groups = heads // per_group
    per_y = groups // y_size
    pieces = per_group // 2
    return pl.pallas_call(
        query_kernel,
        grid=(groups,),
        in_specs=[
            pl.BlockSpec((sources, double, rows), lambda g: (0, 0, 0)),
            pl.BlockSpec((1, double, rows), lambda g: (0, 0, 0)),
            pl.BlockSpec((heads, rows), lambda g: (0, 0)),
            pl.BlockSpec((HD, per_group * rows), lambda g: (0, g)),
            pl.BlockSpec((HD, per_group * rows), lambda g: (0, g)),
        ],
        out_specs=[
            pl.BlockSpec((pieces, 1, rows, 2 * HD), lambda g: (g % per_y, g // per_y, 0, 0)),
            pl.BlockSpec((1, rows, rows), lambda g: (g, 0, 0)),
        ],
        out_shape=[
            jax.ShapeDtypeStruct((z_size, y_size, rows, 2 * HD), F32),
            jax.ShapeDtypeStruct((groups, rows, rows), F32),
        ],
        scratch_shapes=[pltpu.VMEM((heads, rows), F32), pltpu.VMEM((heads, rows), F32)],
        compiler_params=pltpu.CompilerParams(vmem_limit_bytes=LIMIT),
        cost_estimate=pl.CostEstimate(
            flops=4 * heads * rows * HD, bytes_accessed=7 * 2**20, transcendentals=sources * heads * rows
        ),
        name="query_terms",
    )(stats, own, maxima, at, bt)


def image_kernel(core_ref, factor_ref, q_ref, do_ref, e_ref, es_ref, keep_k, keep_v, send_k, send_v):
    heads = q_ref.shape[1] // HD
    wide_rhs, narrow_rhs = [], []
    for h in range(heads):
        w = factor_ref[0, :, h : h + 1]
        wd = factor_ref[0, :, heads + h : heads + h + 1]
        q = head(q_ref, h).astype(F32)
        do = head(do_ref, h).astype(F32)
        wide_rhs.append(jnp.concatenate([(w * do).astype(BF16), (wd * q).astype(BF16)], axis=1))
        narrow_rhs.append((w * q).astype(BF16))
    both = jnp.dot(e_ref[...], jnp.concatenate(wide_rhs, axis=0), preferred_element_type=F32)
    rest = jnp.dot(es_ref[...], jnp.concatenate(narrow_rhs, axis=0), preferred_element_type=F32)
    grad_v = both[:, :HD]
    grad_k = (both[:, HD:] + rest) * SCALE
    even_core = core_ref[0] == 0
    pieces, size = keep_k.shape[0], keep_k.shape[1]
    for grad, keep_out, send_out in ((grad_k, keep_k, send_k), (grad_v, keep_v, send_v)):
        for piece in range(pieces):
            even = grad[2 * piece * size : (2 * piece + 1) * size]
            odd = grad[(2 * piece + 1) * size : (2 * piece + 2) * size]
            keep_out[piece] = jnp.where(even_core, even, odd)
            send_out[piece] = jnp.where(even_core, odd, even)


def image_part(core, factors, queries, grad_out, e, es, pieces):
    rows, width = queries.shape
    image_rows, wide = e.shape
    groups = factors.shape[0]
    per_group = width // groups
    size = image_rows // (2 * pieces)
    out = jax.ShapeDtypeStruct((pieces, size, groups * HD), F32)
    out_spec = pl.BlockSpec((pieces, size, HD), lambda g: (0, 0, g))
    return pl.pallas_call(
        image_kernel,
        grid=(groups,),
        in_specs=[
            pl.BlockSpec(memory_space=pltpu.SMEM),
            pl.BlockSpec((1, rows, rows), lambda g: (g, 0, 0)),
            pl.BlockSpec((rows, per_group), lambda g: (0, g)),
            pl.BlockSpec((rows, per_group), lambda g: (0, g)),
            pl.BlockSpec((image_rows, wide // groups), lambda g: (0, g)),
            pl.BlockSpec((image_rows, wide // groups), lambda g: (0, g)),
        ],
        out_specs=[out_spec] * 4,
        out_shape=[out] * 4,
        compiler_params=pltpu.CompilerParams(vmem_limit_bytes=LIMIT),
        cost_estimate=pl.CostEstimate(
            flops=6 * width * rows * image_rows, bytes_accessed=15 * 2**20, transcendentals=0
        ),
        name="image_terms",
    )(core, factors, queries, grad_out, e, es)


def on_device(queries, keys, values, grad_out, keep_blocks):
    image_size = lax.axis_size("image")
    text_size = lax.axis_size("text")
    y_size = 2
    z_size = image_size // y_size
    pieces = text_size // 2
    z_groups = [[y * z_size + z for z in range(z_size)] for y in range(y_size)]
    core_groups = [[2 * k + c for k in range(pieces)] for c in range(2)]
    image_index = lax.axis_index("image")
    core = lax.axis_index("text") % 2

    e, es, at, bt, own, maxima = local_part(keep_blocks, queries, grad_out, keys, values, image_size)
    stats = lax.all_to_all(own, "image", 0, 0, tiled=True)
    query_terms, factors = query_part(stats, own, maxima, at, bt, z_size, y_size)
    over_z = lax.psum_scatter(
        query_terms, "image", scatter_dimension=0, tiled=True, axis_index_groups=z_groups
    )[0]

    keep_k, keep_v, send_k, send_v = image_part(
        core.astype(jnp.int32).reshape(1), factors, queries, grad_out, e, es, pieces
    )
    swap_core = [(t, t ^ 1) for t in range(text_size)]
    image_terms = jnp.concatenate(
        [keep_k + lax.ppermute(send_k, "text", swap_core), keep_v + lax.ppermute(send_v, "text", swap_core)],
        axis=2,
    )
    arrived = lax.all_to_all(image_terms, "text", 0, 0, tiled=True, axis_index_groups=core_groups)
    image_sum = jnp.sum(arrived, axis=0)
    key_width = keys.shape[1]
    grad_keys = image_sum[:, :key_width].astype(BF16)
    grad_values = image_sum[:, key_width:].astype(BF16)

    mine = image_index // z_size
    own_y = lax.dynamic_index_in_dim(over_z, mine, 0, False)
    other_y = lax.dynamic_index_in_dim(over_z, 1 - mine, 0, False)
    swap_y = [(i, (i + z_size) % image_size) for i in range(image_size)]
    grad_queries = (own_y + lax.ppermute(other_y, "image", swap_y)).astype(BF16)
    return (grad_queries, grad_keys, grad_values)


def solution(mesh):
    return jax.shard_map(
        on_device,
        mesh=mesh,
        in_specs=(
            P("text", None),
            P("image", None),
            P("image", None),
            P("text", None),
            P("text", "image"),
        ),
        out_specs=(P("text", "image"), P(("image", "text"), None), P(("image", "text"), None)),
        check_vma=False,
    )
```

```python
import jax
import jax.numpy as jnp
from jax import lax
from jax.experimental import pallas as pl
from jax.experimental.pallas import tpu as pltpu
from jax.sharding import PartitionSpec as P

HD = 128
TBLK = 64
FBLK = 128
SCALE = HD ** (-0.5)
MASKED = -1e30
NO_KEY = -1e29
LIMIT = 56 * 1024 * 1024

F32 = jnp.float32
BF16 = jnp.bfloat16
LAST = (((1,), (1,)), ((), ()))
FIRST = (((0,), (0,)), ((), ()))


def head(array, index):
    return array[:, index * HD : (index + 1) * HD]


def row_fold(block, combine):
    parts = [block[8 * i : 8 * i + 8] for i in range(block.shape[0] // 8)]
    while len(parts) > 1:
        parts = [combine(parts[i], parts[i + 1]) for i in range(0, len(parts) - 1, 2)] + (
            [parts[-1]] if len(parts) % 2 else []
        )
    return parts[0]


def local_kernel(keep_ref, q_ref, do_ref, k_ref, v_ref, e_ref, stat_ref, max_ref, s_scr, g_scr):
    group = pl.program_id(0)
    heads = q_ref.shape[1] // HD
    rows = q_ref.shape[0]
    blocks = k_ref.shape[0] // FBLK
    copies, stat_rows = stat_ref.shape[0], stat_ref.shape[1] // 2
    first_half = lax.broadcasted_iota(jnp.int32, (1, rows), 1) < TBLK
    bias = [
        jnp.where(
            first_half,
            jnp.where(keep_ref[0, b] > 0, 0.0, MASKED),
            jnp.where(keep_ref[1, b] > 0, 0.0, MASKED),
        ).astype(F32)
        for b in range(blocks)
    ]
    q_all = jnp.concatenate([head(q_ref, h) for h in range(heads)], axis=0)
    do_all = jnp.concatenate([head(do_ref, h) for h in range(heads)], axis=0)
    s_scr[...] = lax.dot_general(k_ref[...], q_all, LAST, preferred_element_type=F32)
    g_scr[...] = lax.dot_general(v_ref[...], do_all, LAST, preferred_element_type=F32)

    def block(h, b):
        return slice(b * FBLK, (b + 1) * FBLK), slice(h * rows, (h + 1) * rows)

    tops = []
    for h in range(heads):
        top = None
        for b in range(blocks):
            part = row_fold(s_scr[block(h, b)], jnp.maximum) + bias[b]
            top = part if top is None else jnp.maximum(top, part)
        tops.append(top)
    row_maxima = [jnp.maximum(jnp.max(top, axis=0, keepdims=True), NO_KEY) for top in tops]
    sums = []
    for h, row_max in enumerate(row_maxima):
        total = jnp.zeros((8, rows), F32)
        product = jnp.zeros((8, rows), F32)
        for b in range(blocks):
            weight = jnp.exp((s_scr[block(h, b)] + (bias[b] - row_max)) * SCALE)
            e_ref[block(h, b)] = weight.astype(BF16)
            total = total + row_fold(weight, jnp.add)
            product = product + row_fold(weight * g_scr[block(h, b)], jnp.add)
        sums.append((total, product))
    maxima, logs, deltas = [], [], []
    for (total, product), row_max in zip(sums, row_maxima):
        total = jnp.sum(total, axis=0, keepdims=True)
        product = jnp.sum(product, axis=0, keepdims=True)
        some = total > 0.0
        safe = jnp.where(some, total, 1.0)
        scaled_max = row_max * SCALE
        maxima.append(scaled_max)
        logs.append(jnp.where(some, scaled_max + jnp.log(safe), MASKED))
        deltas.append(product / safe)
    log_rows = jnp.concatenate(logs, axis=0)
    delta_rows = jnp.concatenate(deltas, axis=0)
    at = pl.multiple_of(group * heads, 8)
    for copy in range(copies):
        stat_ref[copy, pl.ds(at, heads), :] = log_rows
        stat_ref[copy, pl.ds(at + stat_rows, heads), :] = delta_rows
    max_ref[pl.ds(at, heads), :] = jnp.concatenate(maxima, axis=0)


def local_part(keep_blocks, queries, grad_out, keys, values, copies):
    rows, width = queries.shape
    image_rows, key_width = keys.shape
    groups = key_width // HD
    per_group = width // groups
    heads = width // HD
    wide_block = per_group // HD * rows
    return pl.pallas_call(
        local_kernel,
        grid=(groups,),
        in_specs=[
            pl.BlockSpec(memory_space=pltpu.SMEM),
            pl.BlockSpec((rows, per_group), lambda g: (0, g)),
            pl.BlockSpec((rows, per_group), lambda g: (0, g)),
            pl.BlockSpec((image_rows, HD), lambda g: (0, g)),
            pl.BlockSpec((image_rows, HD), lambda g: (0, g)),
        ],
        out_specs=[
            pl.BlockSpec((image_rows, wide_block), lambda g: (0, g)),
            pl.BlockSpec((copies, 2 * heads, rows), lambda g: (0, 0, 0)),
            pl.BlockSpec((heads, rows), lambda g: (0, 0)),
        ],
        out_shape=[
            jax.ShapeDtypeStruct((image_rows, groups * wide_block), BF16),
            jax.ShapeDtypeStruct((copies, 2 * heads, rows), F32),
            jax.ShapeDtypeStruct((heads, rows), F32),
        ],
        scratch_shapes=[
            pltpu.VMEM((image_rows, wide_block), F32),
            pltpu.VMEM((image_rows, wide_block), F32),
        ],
        compiler_params=pltpu.CompilerParams(vmem_limit_bytes=LIMIT),
        cost_estimate=pl.CostEstimate(
            flops=4 * width * rows * image_rows,
            bytes_accessed=9 * 2**20,
            transcendentals=heads * rows * image_rows,
        ),
        name="local_statistics",
    )(keep_blocks, queries, grad_out, keys, values)


def product_kernel(own_ref, do_ref, k_ref, v_ref, e_ref, es_ref, at_ref, bt_ref):
    heads = do_ref.shape[1] // HD
    rows = do_ref.shape[0]
    blocks = k_ref.shape[0] // FBLK
    do_all = jnp.concatenate([head(do_ref, h) for h in range(heads)], axis=0)
    grad_probs = lax.dot_general(v_ref[...], do_all, LAST, preferred_element_type=F32)
    for h in range(heads):
        lanes = slice(h * rows, (h + 1) * rows)
        delta = own_ref[0, h : h + 1, :]
        for b in range(blocks):
            block_rows = slice(b * FBLK, (b + 1) * FBLK)
            centred = (grad_probs[block_rows, lanes] - delta).astype(BF16)
            es_ref[block_rows, lanes] = e_ref[block_rows, lanes] * centred
    at_ref[...] = lax.dot_general(k_ref[...], es_ref[...], FIRST, preferred_element_type=F32)
    bt_ref[...] = lax.dot_general(k_ref[...], e_ref[...], FIRST, preferred_element_type=F32)


def product_part(own, grad_out, keys, values, e):
    rows, width = grad_out.shape
    image_rows, key_width = keys.shape
    groups = key_width // HD
    per_group = width // groups
    heads = per_group // HD
    wide_block = heads * rows
    wide = jax.ShapeDtypeStruct((HD, groups * wide_block), F32)
    return pl.pallas_call(
        product_kernel,
        grid=(groups,),
        in_specs=[
            pl.BlockSpec((1, heads, rows), lambda g: (0, groups + g, 0)),
            pl.BlockSpec((rows, per_group), lambda g: (0, g)),
            pl.BlockSpec((image_rows, HD), lambda g: (0, g)),
            pl.BlockSpec((image_rows, HD), lambda g: (0, g)),
            pl.BlockSpec((image_rows, wide_block), lambda g: (0, g)),
        ],
        out_specs=[
            pl.BlockSpec((image_rows, wide_block), lambda g: (0, g)),
            pl.BlockSpec((HD, wide_block), lambda g: (0, g)),
            pl.BlockSpec((HD, wide_block), lambda g: (0, g)),
        ],
        out_shape=[jax.ShapeDtypeStruct(e.shape, BF16), wide, wide],
        compiler_params=pltpu.CompilerParams(vmem_limit_bytes=LIMIT),
        cost_estimate=pl.CostEstimate(
            flops=6 * width * rows * image_rows, bytes_accessed=18 * 2**20, transcendentals=0
        ),
        name="local_products",
    )(own, grad_out, keys, values, e)


def piece_offsets(z_size):
    half = z_size // 2
    order = [half]
    for distance in range(half - 1, 0, -1):
        order += [-distance, distance]
    return order + [0]


def put_term(out_ref, y_slot, w_pair, d_pair, at_ref, bt_ref):
    rows = at_ref.shape[1] // 2
    for h in range(2):
        lanes = slice(h * rows, (h + 1) * rows)
        total = w_pair[h : h + 1] * at_ref[:, lanes] + d_pair[h : h + 1] * bt_ref[:, lanes]
        out_ref[y_slot, :, h * HD : (h + 1) * HD] = jnp.transpose(total * SCALE)


def merge_kernel(
    place_ref, all_ref, own_ref, max_ref, at0, at1, bt0, bt1,
    right_ref, left_ref, factor_ref, row_ref, row_scr,
):
    step = pl.program_id(0)
    sources, double, rows = all_ref.shape
    heads = double // 2
    pairs = heads // 2
    groups = factor_ref.shape[0]
    per_group = heads // groups

    @pl.when(step == 0)
    def _():
        logs = [all_ref[s, 0:heads, :] for s in range(sources)]
        top = logs[0]
        for log in logs[1:]:
            top = jnp.maximum(top, log)
        total = jnp.zeros((heads, rows), F32)
        product = jnp.zeros((heads, rows), F32)
        for s in range(sources):
            share = jnp.exp(logs[s] - top)
            total = total + share
            product = product + share * all_ref[s, heads:double, :]
        w = jnp.exp(max_ref[...] - (top + jnp.log(total)))
        d = w * (own_ref[0, heads:double, :] - product / total)
        for pair in range(pairs):
            both = jnp.concatenate([w[2 * pair : 2 * pair + 2], d[2 * pair : 2 * pair + 2]], axis=0)
            row_scr[pair, 0:4] = both
            row_ref[pair, 0:4] = both
        fill = jnp.zeros((rows - 2 * per_group, rows), F32)
        for g in range(groups):
            at = slice(g * per_group, (g + 1) * per_group)
            factor_ref[g] = jnp.transpose(jnp.concatenate([w[at], d[at], fill], axis=0))

    offset = jnp.where(step == 0, pairs // 4, pairs // 2 - pairs // 4 + 1)
    for slot, at_ref, bt_ref in ((0, at0, bt0), (1, at1, bt1)):
        pair_rows = row_scr[pair_at(place_ref, offset, slot, pairs)]

        @pl.when(step == 0)
        def _():
            put_term(right_ref, slot, pair_rows[0:2], pair_rows[2:4], at_ref, bt_ref)

        @pl.when(step == 1)
        def _():
            put_term(left_ref, slot, pair_rows[0:2], pair_rows[2:4], at_ref, bt_ref)


def pair_at(place_ref, offset, slot, pairs):
    z_size = pairs // 2
    y = lax.rem(place_ref[0] + slot, 2)
    return y * z_size + lax.rem(place_ref[1] + offset, z_size)


def merge_part(place, stats, own, maxima, at, bt, groups):
    sources, double, rows = stats.shape
    heads = double // 2
    pairs = heads // 2
    z_size = pairs // 2
    first, second = (o % z_size for o in piece_offsets(z_size)[:2])

    def spec(slot):
        def index(s, place):
            return 0, pair_at(place, jnp.where(s == 0, first, second), slot, pairs)

        return pl.BlockSpec((HD, 2 * rows), index)

    piece = jax.ShapeDtypeStruct((2, rows, 2 * HD), F32)
    piece_spec = pl.BlockSpec((2, rows, 2 * HD), lambda s, place: (0, 0, 0))
    grid_spec = pltpu.PrefetchScalarGridSpec(
        num_scalar_prefetch=1,
        grid=(2,),
        in_specs=[
            pl.BlockSpec((sources, double, rows), lambda s, place: (0, 0, 0)),
            pl.BlockSpec((1, double, rows), lambda s, place: (0, 0, 0)),
            pl.BlockSpec((heads, rows), lambda s, place: (0, 0)),
            spec(0), spec(1), spec(0), spec(1),
        ],
        out_specs=[
            piece_spec,
            piece_spec,
            pl.BlockSpec((groups, rows, rows), lambda s, place: (0, 0, 0)),
            pl.BlockSpec((pairs, 8, rows), lambda s, place: (0, 0, 0)),
        ],
        scratch_shapes=[pltpu.VMEM((pairs, 8, rows), F32)],
    )
    return pl.pallas_call(
        merge_kernel,
        grid_spec=grid_spec,
        out_shape=[
            piece,
            piece,
            jax.ShapeDtypeStruct((groups, rows, rows), F32),
            jax.ShapeDtypeStruct((pairs, 8, rows), F32),
        ],
        compiler_params=pltpu.CompilerParams(vmem_limit_bytes=LIMIT),
        cost_estimate=pl.CostEstimate(
            flops=heads * rows * HD, bytes_accessed=3 * 2**20, transcendentals=sources * heads * rows
        ),
        name="merged_statistics",
    )(place, stats, own, maxima, at, at, bt, bt)


def query_kernel(offset_ref, place_ref, row_ref, at0, at1, bt0, bt1, *out_refs):
    step = pl.program_id(0)
    pairs = row_ref.shape[0]
    for slot, at_ref, bt_ref in ((0, at0, bt0), (1, at1, bt1)):
        pair_rows = row_ref[pair_at(place_ref, offset_ref[step], slot, pairs)]
        for index, out_ref in enumerate(out_refs):

            @pl.when(step == index)
            def _(out_ref=out_ref):
                put_term(out_ref, slot, pair_rows[0:2], pair_rows[2:4], at_ref, bt_ref)


def query_part(offsets, place, pair_rows, at, bt):
    pairs, _, rows = pair_rows.shape
    count = offsets.shape[0]

    def spec(slot):
        def index(s, offset, place):
            return 0, pair_at(place, offset[s], slot, pairs)

        return pl.BlockSpec((HD, 2 * rows), index)

    piece_spec = pl.BlockSpec((2, rows, 2 * HD), lambda s, offset, place: (0, 0, 0))
    grid_spec = pltpu.PrefetchScalarGridSpec(
        num_scalar_prefetch=2,
        grid=(count,),
        in_specs=[
            pl.BlockSpec((pairs, 8, rows), lambda s, offset, place: (0, 0, 0)),
            spec(0), spec(1), spec(0), spec(1),
        ],
        out_specs=[piece_spec] * count,
    )
    return pl.pallas_call(
        query_kernel,
        grid_spec=grid_spec,
        out_shape=[jax.ShapeDtypeStruct((2, rows, 2 * HD), F32)] * count,
        compiler_params=pltpu.CompilerParams(vmem_limit_bytes=LIMIT),
        cost_estimate=pl.CostEstimate(
            flops=4 * count * 4 * rows * HD, bytes_accessed=5 * 2**20, transcendentals=0
        ),
        name="query_terms",
    )(offsets, place, pair_rows, at, at, bt, bt)


def image_kernel(core_ref, factor_ref, q_ref, do_ref, e_ref, es_ref, keep_ref, send_ref):
    heads = q_ref.shape[1] // HD
    wide_rhs, narrow_rhs = [], []
    for h in range(heads):
        w = factor_ref[0, :, h : h + 1]
        wd = factor_ref[0, :, heads + h : heads + h + 1]
        q = head(q_ref, h).astype(F32)
        do = head(do_ref, h).astype(F32)
        wide_rhs.append(jnp.concatenate([(w * do).astype(BF16), (wd * q).astype(BF16)], axis=1))
        narrow_rhs.append((w * q).astype(BF16))
    both = jnp.dot(e_ref[...], jnp.concatenate(wide_rhs, axis=0), preferred_element_type=F32)
    rest = jnp.dot(es_ref[...], jnp.concatenate(narrow_rhs, axis=0), preferred_element_type=F32)
    grad_v = both[:, :HD]
    grad_k = (both[:, HD:] + rest) * SCALE
    even_core = core_ref[0] == 0
    pieces, size = keep_ref.shape[0], keep_ref.shape[1]
    for at, grad in ((0, grad_k), (HD, grad_v)):
        for piece in range(pieces):
            even = grad[2 * piece * size : (2 * piece + 1) * size]
            odd = grad[(2 * piece + 1) * size : (2 * piece + 2) * size]
            keep_ref[piece, :, at : at + HD] = jnp.where(even_core, even, odd)
            send_ref[piece, :, at : at + HD] = jnp.where(even_core, odd, even)


def image_part(core, factors, queries, grad_out, e, es, pieces):
    rows, width = queries.shape
    image_rows, wide = e.shape
    groups = factors.shape[0]
    per_group = width // groups
    size = image_rows // (2 * pieces)
    out = jax.ShapeDtypeStruct((pieces, size, groups * 2 * HD), F32)
    out_spec = pl.BlockSpec((pieces, size, 2 * HD), lambda g: (0, 0, g))
    return pl.pallas_call(
        image_kernel,
        grid=(groups,),
        in_specs=[
            pl.BlockSpec(memory_space=pltpu.SMEM),
            pl.BlockSpec((1, rows, rows), lambda g: (g, 0, 0)),
            pl.BlockSpec((rows, per_group), lambda g: (0, g)),
            pl.BlockSpec((rows, per_group), lambda g: (0, g)),
            pl.BlockSpec((image_rows, wide // groups), lambda g: (0, g)),
            pl.BlockSpec((image_rows, wide // groups), lambda g: (0, g)),
        ],
        out_specs=[out_spec] * 2,
        out_shape=[out] * 2,
        compiler_params=pltpu.CompilerParams(vmem_limit_bytes=LIMIT),
        cost_estimate=pl.CostEstimate(
            flops=6 * width * rows * image_rows, bytes_accessed=15 * 2**20, transcendentals=0
        ),
        name="image_terms",
    )(core, factors, queries, grad_out, e, es)


def chain(first_right, first_left, later, axis, z_size, y_size):
    def turn(by):
        return [
            (y * z_size + z, y * z_size + (z + by) % z_size) for y in range(y_size) for z in range(z_size)
        ]

    order = piece_offsets(z_size)[2:]
    term = dict(zip(order, later))
    right = lax.ppermute(first_right, axis, turn(1))
    left = lax.ppermute(first_left, axis, turn(-1))
    for distance in range(z_size // 2 - 1, 0, -1):
        right = lax.ppermute(right + term[distance], axis, turn(1))
        if distance > 1:
            left = lax.ppermute(left + term[1 - distance], axis, turn(-1))
    return left, right, term[0]


def on_device(queries, keys, values, grad_out, keep_blocks):
    image_size = lax.axis_size("image")
    text_size = lax.axis_size("text")
    y_size = 2
    z_size = image_size // y_size
    pieces = text_size // 2
    groups = keys.shape[1] // HD
    core_groups = [[2 * k + c for k in range(pieces)] for c in range(2)]
    swap_y = [(i, (i + z_size) % image_size) for i in range(image_size)]
    swap_core = [(t, t ^ 1) for t in range(text_size)]
    image_index = lax.axis_index("image").astype(jnp.int32)
    place = jnp.stack([image_index // z_size, image_index % z_size])
    offsets = jnp.array([o % z_size for o in piece_offsets(z_size)[2:]], jnp.int32)
    core = (lax.axis_index("text") % 2).astype(jnp.int32).reshape(1)

    e, own, maxima = local_part(keep_blocks, queries, grad_out, keys, values, image_size)
    stats = lax.all_to_all(own, "image", 0, 0, tiled=True)
    es, at, bt = product_part(own, grad_out, keys, values, e)
    first_right, first_left, factors, pair_rows = merge_part(place, stats, own, maxima, at, bt, groups)
    later = query_part(offsets, place, pair_rows, at, bt)
    left, right, here = chain(first_right, first_left, later, "image", z_size, y_size)
    query_sum = left + right + here
    grad_queries = (query_sum[0] + lax.ppermute(query_sum[1], "image", swap_y)).astype(BF16)

    keep, send = image_part(core, factors, queries, grad_out, e, es, pieces)
    image_terms = keep + lax.ppermute(send, "text", swap_core)
    text_arrived = lax.all_to_all(image_terms, "text", 0, 0, tiled=True, axis_index_groups=core_groups)
    image_sum = jnp.sum(text_arrived, axis=0)
    both = image_sum.reshape(image_sum.shape[0], groups, 2, HD)
    grad_keys = both[:, :, 0].reshape(-1, groups * HD).astype(BF16)
    grad_values = both[:, :, 1].reshape(-1, groups * HD).astype(BF16)
    return (grad_queries, grad_keys, grad_values)


def solution(mesh):
    return jax.shard_map(
        on_device,
        mesh=mesh,
        in_specs=(
            P("text", None),
            P("image", None),
            P("image", None),
            P("text", None),
            P("text", "image"),
        ),
        out_specs=(P("text", "image"), P(("image", "text"), None), P(("image", "text"), None)),
        check_vma=False,
    )
```

```python
import jax
import jax.numpy as jnp
from jax import lax
from jax.experimental import pallas as pl
from jax.experimental.pallas import tpu as pltpu
from jax.sharding import PartitionSpec as P

HD = 128
TBLK = 64
FBLK = 128
SCALE = HD ** (-0.5)
MASKED = -1e30
NO_KEY = -1e29
LIMIT = 56 * 1024 * 1024
PRODUCT_LIMIT = 56 * 1024 * 1024
MERGE_LIMIT = 56 * 1024 * 1024
TERM_LIMIT = 56 * 1024 * 1024

F32 = jnp.float32
BF16 = jnp.bfloat16
LAST = (((1,), (1,)), ((), ()))
FIRST = (((0,), (0,)), ((), ()))


def head(array, index):
    return array[:, index * HD : (index + 1) * HD]


def row_fold(block, combine):
    parts = [block[8 * i : 8 * i + 8] for i in range(block.shape[0] // 8)]
    while len(parts) > 1:
        parts = [combine(parts[i], parts[i + 1]) for i in range(0, len(parts) - 1, 2)] + (
            [parts[-1]] if len(parts) % 2 else []
        )
    return parts[0]


def local_kernel(keep_ref, q_ref, do_ref, k_ref, v_ref, e_ref, stat_ref, max_ref, s_scr, g_scr):
    group = pl.program_id(0)
    heads = q_ref.shape[1] // HD
    rows = q_ref.shape[0]
    blocks = k_ref.shape[0] // FBLK
    copies, stat_rows = stat_ref.shape[0], stat_ref.shape[1] // 2
    first_half = lax.broadcasted_iota(jnp.int32, (1, rows), 1) < TBLK
    bias = [
        jnp.where(
            first_half,
            jnp.where(keep_ref[0, b] > 0, 0.0, MASKED),
            jnp.where(keep_ref[1, b] > 0, 0.0, MASKED),
        ).astype(F32)
        for b in range(blocks)
    ]
    q_all = jnp.concatenate([head(q_ref, h) for h in range(heads)], axis=0)
    do_all = jnp.concatenate([head(do_ref, h) for h in range(heads)], axis=0)
    s_scr[...] = lax.dot_general(k_ref[...], q_all, LAST, preferred_element_type=F32)
    g_scr[...] = lax.dot_general(v_ref[...], do_all, LAST, preferred_element_type=F32)

    def block(h, b):
        return slice(b * FBLK, (b + 1) * FBLK), slice(h * rows, (h + 1) * rows)

    tops = []
    for h in range(heads):
        top = None
        for b in range(blocks):
            part = row_fold(s_scr[block(h, b)], jnp.maximum) + bias[b]
            top = part if top is None else jnp.maximum(top, part)
        tops.append(top)
    row_maxima = [jnp.maximum(jnp.max(top, axis=0, keepdims=True), NO_KEY) for top in tops]
    sums = []
    for h, row_max in enumerate(row_maxima):
        total = jnp.zeros((8, rows), F32)
        product = jnp.zeros((8, rows), F32)
        for b in range(blocks):
            weight = jnp.exp((s_scr[block(h, b)] + (bias[b] - row_max)) * SCALE)
            e_ref[block(h, b)] = weight.astype(BF16)
            total = total + row_fold(weight, jnp.add)
            product = product + row_fold(weight * g_scr[block(h, b)], jnp.add)
        sums.append((total, product))
    maxima, logs, deltas = [], [], []
    for (total, product), row_max in zip(sums, row_maxima):
        total = jnp.sum(total, axis=0, keepdims=True)
        product = jnp.sum(product, axis=0, keepdims=True)
        some = total > 0.0
        safe = jnp.where(some, total, 1.0)
        scaled_max = row_max * SCALE
        maxima.append(scaled_max)
        logs.append(jnp.where(some, scaled_max + jnp.log(safe), MASKED))
        deltas.append(product / safe)
    log_rows = jnp.concatenate(logs, axis=0)
    delta_rows = jnp.concatenate(deltas, axis=0)
    at = pl.multiple_of(group * heads, 8)
    for copy in range(copies):
        stat_ref[copy, pl.ds(at, heads), :] = log_rows
        stat_ref[copy, pl.ds(at + stat_rows, heads), :] = delta_rows
    max_ref[pl.ds(at, heads), :] = jnp.concatenate(maxima, axis=0)


def local_part(keep_blocks, queries, grad_out, keys, values, copies):
    rows, width = queries.shape
    image_rows, key_width = keys.shape
    groups = key_width // HD
    per_group = width // groups
    heads = width // HD
    wide_block = per_group // HD * rows
    return pl.pallas_call(
        local_kernel,
        grid=(groups,),
        in_specs=[
            pl.BlockSpec(memory_space=pltpu.SMEM),
            pl.BlockSpec((rows, per_group), lambda g: (0, g)),
            pl.BlockSpec((rows, per_group), lambda g: (0, g)),
            pl.BlockSpec((image_rows, HD), lambda g: (0, g)),
            pl.BlockSpec((image_rows, HD), lambda g: (0, g)),
        ],
        out_specs=[
            pl.BlockSpec((image_rows, wide_block), lambda g: (0, g)),
            pl.BlockSpec((copies, 2 * heads, rows), lambda g: (0, 0, 0)),
            pl.BlockSpec((heads, rows), lambda g: (0, 0)),
        ],
        out_shape=[
            jax.ShapeDtypeStruct((image_rows, groups * wide_block), BF16),
            jax.ShapeDtypeStruct((copies, 2 * heads, rows), F32),
            jax.ShapeDtypeStruct((heads, rows), F32),
        ],
        scratch_shapes=[
            pltpu.VMEM((image_rows, wide_block), F32),
            pltpu.VMEM((image_rows, wide_block), F32),
        ],
        compiler_params=pltpu.CompilerParams(vmem_limit_bytes=LIMIT),
        cost_estimate=pl.CostEstimate(
            flops=4 * width * rows * image_rows,
            bytes_accessed=9 * 2**20,
            transcendentals=heads * rows * image_rows,
        ),
        name="local_statistics",
    )(keep_blocks, queries, grad_out, keys, values)


def product_kernel(own_ref, do_ref, k_ref, v_ref, e_ref, es_ref, at_ref, bt_ref):
    heads = do_ref.shape[1] // HD
    rows = do_ref.shape[0]
    blocks = k_ref.shape[0] // FBLK
    do_all = jnp.concatenate([head(do_ref, h) for h in range(heads)], axis=0)
    grad_probs = lax.dot_general(v_ref[...], do_all, LAST, preferred_element_type=F32)
    for h in range(heads):
        lanes = slice(h * rows, (h + 1) * rows)
        delta = own_ref[0, h : h + 1, :]
        for b in range(blocks):
            block_rows = slice(b * FBLK, (b + 1) * FBLK)
            centred = grad_probs[block_rows, lanes] - delta
            es_ref[block_rows, lanes] = (e_ref[block_rows, lanes].astype(F32) * centred).astype(BF16)
    at_ref[...] = lax.dot_general(k_ref[...], es_ref[...], FIRST, preferred_element_type=F32)
    bt_ref[...] = lax.dot_general(k_ref[...], e_ref[...], FIRST, preferred_element_type=F32)


def product_part(own, grad_out, keys, values, e):
    rows, width = grad_out.shape
    image_rows, key_width = keys.shape
    groups = key_width // HD
    per_group = width // groups
    heads = per_group // HD
    wide_block = heads * rows
    wide = jax.ShapeDtypeStruct((HD, groups * wide_block), F32)
    return pl.pallas_call(
        product_kernel,
        grid=(groups,),
        in_specs=[
            pl.BlockSpec((1, heads, rows), lambda g: (0, groups + g, 0)),
            pl.BlockSpec((rows, per_group), lambda g: (0, g)),
            pl.BlockSpec((image_rows, HD), lambda g: (0, g)),
            pl.BlockSpec((image_rows, HD), lambda g: (0, g)),
            pl.BlockSpec((image_rows, wide_block), lambda g: (0, g)),
        ],
        out_specs=[
            pl.BlockSpec((image_rows, wide_block), lambda g: (0, g)),
            pl.BlockSpec((HD, wide_block), lambda g: (0, g)),
            pl.BlockSpec((HD, wide_block), lambda g: (0, g)),
        ],
        out_shape=[jax.ShapeDtypeStruct(e.shape, BF16), wide, wide],
        compiler_params=pltpu.CompilerParams(vmem_limit_bytes=PRODUCT_LIMIT),
        cost_estimate=pl.CostEstimate(
            flops=6 * width * rows * image_rows, bytes_accessed=18 * 2**20, transcendentals=0
        ),
        name="local_products",
    )(own, grad_out, keys, values, e)


def piece_offsets(z_size):
    half = z_size // 2
    order = [half]
    for distance in range(half - 1, 0, -1):
        order += [-distance, distance]
    return order + [0]


def put_term(out_ref, y_slot, factor_ref, pair, at_ref, bt_ref):
    rows = at_ref.shape[1] // 2
    for h in range(2):
        lanes = slice(h * rows, (h + 1) * rows)
        w_row = factor_ref[0, pl.ds(2 * pair + h, 1), :]
        d_row = factor_ref[1, pl.ds(2 * pair + h, 1), :]
        out_ref[y_slot, :, h * HD : (h + 1) * HD] = jnp.transpose(
            w_row * at_ref[:, lanes] + d_row * bt_ref[:, lanes]
        )


def merge_kernel(
    place_ref, all_ref, own_ref, max_ref, at0, at1, bt0, bt1, right_ref, left_ref, factor_ref, row_scr
):
    step = pl.program_id(0)
    sources, double, rows = all_ref.shape
    heads = double // 2
    pairs = heads // 2

    @pl.when(step == 0)
    def _():
        logs = [all_ref[s, 0:heads, :] for s in range(sources)]
        top = logs[0]
        for log in logs[1:]:
            top = jnp.maximum(top, log)
        total = jnp.zeros((heads, rows), F32)
        product = jnp.zeros((heads, rows), F32)
        for s in range(sources):
            share = jnp.exp(logs[s] - top)
            total = total + share
            product = product + share * all_ref[s, heads:double, :]
        w = jnp.exp(max_ref[...] - (top + jnp.log(total)))
        d = w * (own_ref[0, heads:double, :] - product / total)
        factor_ref[0] = w
        factor_ref[1] = d
        row_scr[0] = w * SCALE
        row_scr[1] = d * SCALE

    offset = jnp.where(step == 0, pairs // 4, pairs // 2 - pairs // 4 + 1)
    for slot, at_ref, bt_ref in ((0, at0, bt0), (1, at1, bt1)):
        pair = pair_at(place_ref, offset, slot, pairs)

        @pl.when(step == 0)
        def _():
            put_term(right_ref, slot, row_scr, pair, at_ref, bt_ref)

        @pl.when(step == 1)
        def _():
            put_term(left_ref, slot, row_scr, pair, at_ref, bt_ref)


def pair_at(place_ref, offset, slot, pairs):
    z_size = pairs // 2
    y = lax.rem(place_ref[0] + slot, 2)
    return y * z_size + lax.rem(place_ref[1] + offset, z_size)


def merge_part(place, stats, own, maxima, at, bt):
    sources, double, rows = stats.shape
    heads = double // 2
    pairs = heads // 2
    z_size = pairs // 2
    first, second = (o % z_size for o in piece_offsets(z_size)[:2])

    def spec(slot):
        def index(s, place):
            return 0, pair_at(place, jnp.where(s == 0, first, second), slot, pairs)

        return pl.BlockSpec((HD, 2 * rows), index)

    piece = jax.ShapeDtypeStruct((2, rows, 2 * HD), F32)
    piece_spec = pl.BlockSpec((2, rows, 2 * HD), lambda s, place: (0, 0, 0))
    grid_spec = pltpu.PrefetchScalarGridSpec(
        num_scalar_prefetch=1,
        grid=(2,),
        in_specs=[
            pl.BlockSpec((sources, double, rows), lambda s, place: (0, 0, 0)),
            pl.BlockSpec((1, double, rows), lambda s, place: (0, 0, 0)),
            pl.BlockSpec((heads, rows), lambda s, place: (0, 0)),
            spec(0), spec(1), spec(0), spec(1),
        ],
        out_specs=[
            piece_spec,
            piece_spec,
            pl.BlockSpec((2, heads, rows), lambda s, place: (0, 0, 0)),
        ],
        scratch_shapes=[pltpu.VMEM((2, heads, rows), F32)],
    )
    return pl.pallas_call(
        merge_kernel,
        grid_spec=grid_spec,
        out_shape=[
            piece,
            piece,
            jax.ShapeDtypeStruct((2, heads, rows), F32),
        ],
        compiler_params=pltpu.CompilerParams(vmem_limit_bytes=MERGE_LIMIT),
        cost_estimate=pl.CostEstimate(
            flops=heads * rows * HD, bytes_accessed=3 * 2**20, transcendentals=sources * heads * rows
        ),
        name="merged_statistics",
    )(place, stats, own, maxima, at, at, bt, bt)


def term_kernel(
    offset_ref, place_ref, core_ref, all_factor_ref, factor_ref, q_ref, do_ref, e_ref, es_ref,
    at00, at01, at10, at11, bt00, bt01, bt10, bt11, term_ref, keep_ref, send_ref, row_scr,
):
    step = pl.program_id(0)
    pairs = all_factor_ref.shape[1] // 2

    @pl.when(step == 0)
    def _():
        row_scr[...] = all_factor_ref[...] * SCALE

    for i, blocks in enumerate((((at00, bt00), (at01, bt01)), ((at10, bt10), (at11, bt11)))):
        for slot, (at_ref, bt_ref) in enumerate(blocks):
            pair = pair_at(place_ref, offset_ref[2 * step + i], slot, pairs)
            put_term(term_ref.at[i], slot, row_scr, pair, at_ref, bt_ref)

    heads = q_ref.shape[1] // HD
    rows = q_ref.shape[0]
    fill = jnp.zeros((rows - 2 * heads, rows), F32)
    columns = jnp.transpose(jnp.concatenate([factor_ref[0], factor_ref[1], fill], axis=0))
    wide_rhs, narrow_rhs = [], []
    for h in range(heads):
        w = columns[:, h : h + 1]
        wd = columns[:, heads + h : heads + h + 1]
        q = head(q_ref, h).astype(F32)
        do = head(do_ref, h).astype(F32)
        wide_rhs.append(jnp.concatenate([(w * do).astype(BF16), (wd * q).astype(BF16)], axis=1))
        narrow_rhs.append((w * q).astype(BF16))
    both = jnp.dot(e_ref[...], jnp.concatenate(wide_rhs, axis=0), preferred_element_type=F32)
    rest = jnp.dot(es_ref[...], jnp.concatenate(narrow_rhs, axis=0), preferred_element_type=F32)
    grad_v = both[:, :HD]
    grad_k = (both[:, HD:] + rest) * SCALE
    even_core = core_ref[0] == 0
    pieces, size = keep_ref.shape[0], keep_ref.shape[1]
    for at, grad in ((0, grad_k), (HD, grad_v)):
        for piece in range(pieces):
            even = grad[2 * piece * size : (2 * piece + 1) * size]
            odd = grad[(2 * piece + 1) * size : (2 * piece + 2) * size]
            y, x = divmod(piece, pieces // 2)
            x_offset = lax.rem(x + pieces // 2 - core_ref[2], pieces // 2)
            slot = 2 * x_offset + lax.rem(core_ref[1] + y, 2)
            keep_ref[slot, :, at : at + HD] = jnp.where(even_core, even, odd)
            send_ref[slot, :, at : at + HD] = jnp.where(even_core, odd, even)


def term_part(order, place, core, factors, queries, grad_out, e, es, at, bt, pieces):
    rows, width = queries.shape
    image_rows, wide = e.shape
    heads = factors.shape[1]
    pairs = heads // 2
    groups = heads // 8
    per_group = width // groups
    size = image_rows // (2 * pieces)
    order = [o % (pairs // 2) for o in order]
    offsets = jnp.array(order + order[-2:], jnp.int32)

    def spec(i, slot):
        def index(g, offset, place, core):
            return 0, pair_at(place, offset[2 * g + i], slot, pairs)

        return pl.BlockSpec((HD, 2 * rows), index)

    four = [spec(i, slot) for i in range(2) for slot in range(2)]
    half = jax.ShapeDtypeStruct((pieces, size, groups * 2 * HD), F32)
    half_spec = pl.BlockSpec((pieces, size, 2 * HD), lambda g, *_: (0, 0, g))
    grid_spec = pltpu.PrefetchScalarGridSpec(
        num_scalar_prefetch=3,
        grid=(groups,),
        in_specs=[
            pl.BlockSpec((2, heads, rows), lambda g, *_: (0, 0, 0)),
            pl.BlockSpec((2, heads // groups, rows), lambda g, *_: (0, g, 0)),
            pl.BlockSpec((rows, per_group), lambda g, *_: (0, g)),
            pl.BlockSpec((rows, per_group), lambda g, *_: (0, g)),
            pl.BlockSpec((image_rows, wide // groups), lambda g, *_: (0, g)),
            pl.BlockSpec((image_rows, wide // groups), lambda g, *_: (0, g)),
            *four,
            *four,
        ],
        out_specs=[pl.BlockSpec((2, 2, rows, 2 * HD), lambda g, *_: (g, 0, 0, 0)), half_spec, half_spec],
        scratch_shapes=[pltpu.VMEM((2, heads, rows), F32)],
    )
    return pl.pallas_call(
        term_kernel,
        grid_spec=grid_spec,
        out_shape=[jax.ShapeDtypeStruct((2 * groups, 2, rows, 2 * HD), F32), half, half],
        compiler_params=pltpu.CompilerParams(vmem_limit_bytes=TERM_LIMIT),
        cost_estimate=pl.CostEstimate(
            flops=6 * width * rows * image_rows, bytes_accessed=20 * 2**20, transcendentals=0
        ),
        name="query_and_image_terms",
    )(offsets, place, core, factors, factors, queries, grad_out, e, es, *[at] * 4, *[bt] * 4)


def on_device(queries, keys, values, grad_out, keep_blocks):
    image_size = lax.axis_size("image")
    text_size = lax.axis_size("text")
    y_size = 2
    z_size = image_size // y_size
    pieces = text_size // 2
    groups = keys.shape[1] // HD
    swap_far = [(t, (t + pieces) % text_size) for t in range(text_size)]
    swap_core = [(t, t ^ 1) for t in range(text_size)]
    image_index = lax.axis_index("image").astype(jnp.int32)
    place = jnp.stack([image_index // z_size, image_index % z_size])
    text_index = lax.axis_index("text").astype(jnp.int32)
    x_size = pieces // 2
    core = jnp.stack([text_index % 2, text_index // pieces, text_index // 2 % x_size])

    def turn_x(by):
        return [
            (y * pieces + 2 * x + c, y * pieces + (2 * x + 2 * by) % pieces + c)
            for y in range(2)
            for x in range(x_size)
            for c in range(2)
        ]

    def turn(by, across=0):
        return [
            (y * z_size + z, (y + across) % y_size * z_size + (z + by) % z_size)
            for y in range(y_size)
            for z in range(z_size)
        ]

    e, own, maxima = local_part(keep_blocks, queries, grad_out, keys, values, image_size)
    stats = lax.all_to_all(own, "image", 0, 0, tiled=True)
    es, at, bt = product_part(own, grad_out, keys, values, e)

    first_right, first_left, factors = merge_part(place, stats, own, maxima, at, bt)
    right = lax.ppermute(first_right, "image", turn(1))
    left = lax.ppermute(first_left, "image", turn(-1))
    order = piece_offsets(z_size)[2:]
    terms, keep, send = term_part(
        order, place, core, factors, queries, grad_out, e, es, at, bt, pieces
    )
    terms, keep, send, right, left = lax.optimization_barrier((terms, keep, send, right, left))
    term = {offset: terms[i] for i, offset in enumerate(order)}
    received = lax.ppermute(send, "text", swap_core)
    right = lax.ppermute(right + term[3], "image", turn(1))
    left = lax.ppermute(left + term[-2], "image", turn(-1))
    image_terms = keep + received
    part = [image_terms[2 * by : 2 * by + 2] for by in range(x_size)]
    x_right = lax.ppermute(part[2][0], "text", turn_x(1))
    x_left = lax.ppermute(part[2][1], "text", turn_x(-1))
    right, left, x_right, x_left = lax.optimization_barrier((right, left, x_right, x_left))
    right = lax.ppermute(right + term[2], "image", turn(1))
    left = lax.ppermute(left + term[-1], "image", turn(-1))
    x_right = lax.ppermute(jnp.stack([part[1][0] + x_right, part[1][1]]), "text", turn_x(1))
    x_left = lax.ppermute(jnp.stack([part[3][0], part[3][1] + x_left]), "text", turn_x(-1))
    right, left = lax.optimization_barrier((right, left))
    x_sum = part[0] + x_right + x_left
    image_sum = x_sum[0] + lax.ppermute(x_sum[1], "text", swap_far)
    over = right + term[1]
    here = left + term[0]
    query_sum = (
        here[0]
        + lax.ppermute(over[0], "image", turn(1))
        + lax.ppermute(over[1], "image", turn(1, 1))
        + lax.ppermute(here[1], "image", turn(0, 1))
    )
    grad_queries = query_sum.astype(BF16)
    grad_keys = jnp.concatenate([head(image_sum, 2 * g) for g in range(groups)], axis=1).astype(BF16)
    grad_values = jnp.concatenate([head(image_sum, 2 * g + 1) for g in range(groups)], axis=1).astype(BF16)
    return (grad_queries, grad_keys, grad_values)


def solution(mesh):
    return jax.shard_map(
        on_device,
        mesh=mesh,
        in_specs=(
            P("text", None),
            P("image", None),
            P("image", None),
            P("text", None),
            P("text", "image"),
        ),
        out_specs=(P("text", "image"), P(("image", "text"), None), P(("image", "text"), None)),
        check_vma=False,
    )
```

```python
import jax
import jax.numpy as jnp
from jax import lax
from jax.experimental import pallas as pl
from jax.experimental.pallas import tpu as pltpu
from jax.sharding import PartitionSpec as P

HD = 128
TBLK = 64
FBLK = 128
SCALE = HD ** (-0.5)
MASKED = -1e30
NO_KEY = -1e29
LIMIT = 56 * 1024 * 1024
PRODUCT_LIMIT = 56 * 1024 * 1024
MERGE_LIMIT = 56 * 1024 * 1024
TERM_LIMIT = 56 * 1024 * 1024

F32 = jnp.float32
BF16 = jnp.bfloat16
LAST = (((1,), (1,)), ((), ()))
FIRST = (((0,), (0,)), ((), ()))


def head(array, index):
    return array[:, index * HD : (index + 1) * HD]


def row_fold(block, combine):
    parts = [block[8 * i : 8 * i + 8] for i in range(block.shape[0] // 8)]
    while len(parts) > 1:
        parts = [combine(parts[i], parts[i + 1]) for i in range(0, len(parts) - 1, 2)] + (
            [parts[-1]] if len(parts) % 2 else []
        )
    return parts[0]


def local_kernel(keep_ref, q_ref, do_ref, k_ref, v_ref, e_ref, stat_ref, max_ref, s_scr, g_scr):
    group = pl.program_id(0)
    heads = q_ref.shape[1] // HD
    rows = q_ref.shape[0]
    blocks = k_ref.shape[0] // FBLK
    copies, stat_rows = stat_ref.shape[0], stat_ref.shape[1] // 2
    first_half = lax.broadcasted_iota(jnp.int32, (1, rows), 1) < TBLK
    bias = [
        jnp.where(
            first_half,
            jnp.where(keep_ref[0, b] > 0, 0.0, MASKED),
            jnp.where(keep_ref[1, b] > 0, 0.0, MASKED),
        ).astype(F32)
        for b in range(blocks)
    ]
    q_all = jnp.concatenate([head(q_ref, h) for h in range(heads)], axis=0)
    do_all = jnp.concatenate([head(do_ref, h) for h in range(heads)], axis=0)
    s_scr[...] = lax.dot_general(k_ref[...], q_all, LAST, preferred_element_type=F32)
    g_scr[...] = lax.dot_general(v_ref[...], do_all, LAST, preferred_element_type=F32)

    def block(h, b):
        return slice(b * FBLK, (b + 1) * FBLK), slice(h * rows, (h + 1) * rows)

    tops = []
    for h in range(heads):
        top = None
        for b in range(blocks):
            part = row_fold(s_scr[block(h, b)], jnp.maximum) + bias[b]
            top = part if top is None else jnp.maximum(top, part)
        tops.append(top)
    row_maxima = [jnp.maximum(jnp.max(top, axis=0, keepdims=True), NO_KEY) for top in tops]
    sums = []
    for h, row_max in enumerate(row_maxima):
        total = jnp.zeros((8, rows), F32)
        product = jnp.zeros((8, rows), F32)
        for b in range(blocks):
            weight = jnp.exp((s_scr[block(h, b)] + (bias[b] - row_max)) * SCALE)
            e_ref[block(h, b)] = weight.astype(BF16)
            total = total + row_fold(weight, jnp.add)
            product = product + row_fold(weight * g_scr[block(h, b)], jnp.add)
        sums.append((total, product))
    maxima, logs, deltas = [], [], []
    for (total, product), row_max in zip(sums, row_maxima):
        total = jnp.sum(total, axis=0, keepdims=True)
        product = jnp.sum(product, axis=0, keepdims=True)
        some = total > 0.0
        safe = jnp.where(some, total, 1.0)
        scaled_max = row_max * SCALE
        maxima.append(scaled_max)
        logs.append(jnp.where(some, scaled_max + jnp.log(safe), MASKED))
        deltas.append(product / safe)
    log_rows = jnp.concatenate(logs, axis=0)
    delta_rows = jnp.concatenate(deltas, axis=0)
    at = pl.multiple_of(group * heads, 8)
    for copy in range(copies):
        stat_ref[copy, pl.ds(at, heads), :] = log_rows
        stat_ref[copy, pl.ds(at + stat_rows, heads), :] = delta_rows
    max_ref[pl.ds(at, heads), :] = jnp.concatenate(maxima, axis=0)


def local_part(keep_blocks, queries, grad_out, keys, values, copies):
    rows, width = queries.shape
    image_rows, key_width = keys.shape
    groups = key_width // HD
    per_group = width // groups
    heads = width // HD
    wide_block = per_group // HD * rows
    return pl.pallas_call(
        local_kernel,
        grid=(groups,),
        in_specs=[
            pl.BlockSpec(memory_space=pltpu.SMEM),
            pl.BlockSpec((rows, per_group), lambda g: (0, g)),
            pl.BlockSpec((rows, per_group), lambda g: (0, g)),
            pl.BlockSpec((image_rows, HD), lambda g: (0, g)),
            pl.BlockSpec((image_rows, HD), lambda g: (0, g)),
        ],
        out_specs=[
            pl.BlockSpec((image_rows, wide_block), lambda g: (0, g)),
            pl.BlockSpec((copies, 2 * heads, rows), lambda g: (0, 0, 0)),
            pl.BlockSpec((heads, rows), lambda g: (0, 0)),
        ],
        out_shape=[
            jax.ShapeDtypeStruct((image_rows, groups * wide_block), BF16),
            jax.ShapeDtypeStruct((copies, 2 * heads, rows), F32),
            jax.ShapeDtypeStruct((heads, rows), F32),
        ],
        scratch_shapes=[
            pltpu.VMEM((image_rows, wide_block), F32),
            pltpu.VMEM((image_rows, wide_block), F32),
        ],
        compiler_params=pltpu.CompilerParams(vmem_limit_bytes=LIMIT),
        cost_estimate=pl.CostEstimate(
            flops=4 * width * rows * image_rows,
            bytes_accessed=9 * 2**20,
            transcendentals=heads * rows * image_rows,
        ),
        name="local_statistics",
    )(keep_blocks, queries, grad_out, keys, values)


def product_kernel(own_ref, do_ref, k_ref, v_ref, e_ref, es_ref, at_ref, bt_ref):
    heads = do_ref.shape[1] // HD
    rows = do_ref.shape[0]
    blocks = k_ref.shape[0] // FBLK
    do_all = jnp.concatenate([head(do_ref, h) for h in range(heads)], axis=0)
    grad_probs = lax.dot_general(v_ref[...], do_all, LAST, preferred_element_type=F32)
    for h in range(heads):
        lanes = slice(h * rows, (h + 1) * rows)
        delta = own_ref[0, h : h + 1, :]
        for b in range(blocks):
            block_rows = slice(b * FBLK, (b + 1) * FBLK)
            centred = grad_probs[block_rows, lanes] - delta
            es_ref[block_rows, lanes] = (e_ref[block_rows, lanes].astype(F32) * centred).astype(BF16)
    at_ref[...] = lax.dot_general(k_ref[...], es_ref[...], FIRST, preferred_element_type=F32)
    bt_ref[...] = lax.dot_general(k_ref[...], e_ref[...], FIRST, preferred_element_type=F32)


def product_part(own, grad_out, keys, values, e):
    rows, width = grad_out.shape
    image_rows, key_width = keys.shape
    groups = key_width // HD
    per_group = width // groups
    heads = per_group // HD
    wide_block = heads * rows
    wide = jax.ShapeDtypeStruct((HD, groups * wide_block), F32)
    return pl.pallas_call(
        product_kernel,
        grid=(groups,),
        in_specs=[
            pl.BlockSpec((1, heads, rows), lambda g: (0, groups + g, 0)),
            pl.BlockSpec((rows, per_group), lambda g: (0, g)),
            pl.BlockSpec((image_rows, HD), lambda g: (0, g)),
            pl.BlockSpec((image_rows, HD), lambda g: (0, g)),
            pl.BlockSpec((image_rows, wide_block), lambda g: (0, g)),
        ],
        out_specs=[
            pl.BlockSpec((image_rows, wide_block), lambda g: (0, g)),
            pl.BlockSpec((HD, wide_block), lambda g: (0, g)),
            pl.BlockSpec((HD, wide_block), lambda g: (0, g)),
        ],
        out_shape=[jax.ShapeDtypeStruct(e.shape, BF16), wide, wide],
        compiler_params=pltpu.CompilerParams(vmem_limit_bytes=PRODUCT_LIMIT),
        cost_estimate=pl.CostEstimate(
            flops=6 * width * rows * image_rows, bytes_accessed=18 * 2**20, transcendentals=0
        ),
        name="local_products",
    )(own, grad_out, keys, values, e)


def piece_offsets(z_size):
    half = z_size // 2
    order = [half]
    for distance in range(half - 1, 0, -1):
        order += [-distance, distance]
    return order + [0]


def put_term(out_ref, y_slot, factor_ref, pair, at_ref, bt_ref):
    rows = at_ref.shape[1] // 2
    for h in range(2):
        lanes = slice(h * rows, (h + 1) * rows)
        w_row = factor_ref[0, pl.ds(2 * pair + h, 1), :]
        d_row = factor_ref[1, pl.ds(2 * pair + h, 1), :]
        out_ref[y_slot, :, h * HD : (h + 1) * HD] = jnp.transpose(
            w_row * at_ref[:, lanes] + d_row * bt_ref[:, lanes]
        )


def merge_kernel(
    place_ref, all_ref, own_ref, max_ref, at00, at01, at10, at11, bt00, bt01, bt10, bt11,
    right_ref, left_ref, factor_ref, row_scr,
):
    sources, double, rows = all_ref.shape
    heads = double // 2
    pairs = heads // 2

    logs = [all_ref[s, 0:heads, :] for s in range(sources)]
    top = logs[0]
    for log in logs[1:]:
        top = jnp.maximum(top, log)
    total = jnp.zeros((heads, rows), F32)
    product = jnp.zeros((heads, rows), F32)
    for s in range(sources):
        share = jnp.exp(logs[s] - top)
        total = total + share
        product = product + share * all_ref[s, heads:double, :]
    w = jnp.exp(max_ref[...] - (top + jnp.log(total)))
    d = w * (own_ref[0, heads:double, :] - product / total)
    factor_ref[0] = w
    factor_ref[1] = d
    row_scr[0] = w * SCALE
    row_scr[1] = d * SCALE
    z_size = pairs // 2
    first, second = (o % z_size for o in piece_offsets(z_size)[:2])
    for slot, at_ref, bt_ref in ((0, at00, bt00), (1, at01, bt01)):
        put_term(right_ref, slot, row_scr, pair_at(place_ref, first, slot, pairs), at_ref, bt_ref)
    for slot, at_ref, bt_ref in ((0, at10, bt10), (1, at11, bt11)):
        put_term(left_ref, slot, row_scr, pair_at(place_ref, second, slot, pairs), at_ref, bt_ref)


def pair_at(place_ref, offset, slot, pairs):
    z_size = pairs // 2
    y = lax.rem(place_ref[0] + slot, 2)
    return y * z_size + lax.rem(place_ref[1] + offset, z_size)


def merge_part(place, stats, own, maxima, at, bt):
    sources, double, rows = stats.shape
    heads = double // 2
    pairs = heads // 2
    z_size = pairs // 2

    def spec(offset, slot):
        return pl.BlockSpec(
            (HD, 2 * rows), lambda s, place: (0, pair_at(place, offset, slot, pairs))
        )

    four = [
        spec(offset % z_size, slot) for offset in piece_offsets(z_size)[:2] for slot in range(2)
    ]
    piece = jax.ShapeDtypeStruct((2, rows, 2 * HD), F32)
    piece_spec = pl.BlockSpec((2, rows, 2 * HD), lambda s, place: (0, 0, 0))
    grid_spec = pltpu.PrefetchScalarGridSpec(
        num_scalar_prefetch=1,
        grid=(1,),
        in_specs=[
            pl.BlockSpec((sources, double, rows), lambda s, place: (0, 0, 0)),
            pl.BlockSpec((1, double, rows), lambda s, place: (0, 0, 0)),
            pl.BlockSpec((heads, rows), lambda s, place: (0, 0)),
            *four,
            *four,
        ],
        out_specs=[
            piece_spec,
            piece_spec,
            pl.BlockSpec((2, heads, rows), lambda s, place: (0, 0, 0)),
        ],
        scratch_shapes=[pltpu.VMEM((2, heads, rows), F32)],
    )
    return pl.pallas_call(
        merge_kernel,
        grid_spec=grid_spec,
        out_shape=[
            piece,
            piece,
            jax.ShapeDtypeStruct((2, heads, rows), F32),
        ],
        compiler_params=pltpu.CompilerParams(vmem_limit_bytes=MERGE_LIMIT),
        cost_estimate=pl.CostEstimate(
            flops=heads * rows * HD, bytes_accessed=3 * 2**20, transcendentals=sources * heads * rows
        ),
        name="merged_statistics",
    )(place, stats, own, maxima, *[at] * 4, *[bt] * 4)


def term_kernel(
    offset_ref, place_ref, all_factor_ref, factor_ref, q_ref, do_ref, e_ref, es_ref,
    at00, at01, at10, at11, bt00, bt01, bt10, bt11, term_ref, keep_ref, send_ref, row_scr,
):
    step = pl.program_id(0)
    pairs = all_factor_ref.shape[1] // 2

    @pl.when(step == 0)
    def _():
        row_scr[...] = all_factor_ref[...] * SCALE

    for i, blocks in enumerate((((at00, bt00), (at01, bt01)), ((at10, bt10), (at11, bt11)))):
        for slot, (at_ref, bt_ref) in enumerate(blocks):
            pair = pair_at(place_ref, offset_ref[2 * step + i], slot, pairs)
            put_term(term_ref.at[i], slot, row_scr, pair, at_ref, bt_ref)

    heads = q_ref.shape[1] // HD
    rows = q_ref.shape[0]
    fill = jnp.zeros((rows - 2 * heads, rows), F32)
    columns = jnp.transpose(jnp.concatenate([factor_ref[0], factor_ref[1], fill], axis=0))
    wide_rhs, narrow_rhs = [], []
    for h in range(heads):
        w = columns[:, h : h + 1]
        wd = columns[:, heads + h : heads + h + 1]
        q = head(q_ref, h).astype(F32)
        do = head(do_ref, h).astype(F32)
        wide_rhs.append(jnp.concatenate([(w * do).astype(BF16), (wd * q).astype(BF16)], axis=1))
        narrow_rhs.append((w * q).astype(BF16))
    both = jnp.dot(e_ref[...], jnp.concatenate(wide_rhs, axis=0), preferred_element_type=F32)
    rest = jnp.dot(es_ref[...], jnp.concatenate(narrow_rhs, axis=0), preferred_element_type=F32)
    grad_v = both[:, :HD]
    grad_k = (both[:, HD:] + rest) * SCALE
    even_core = place_ref[2] == 0
    pieces, size = keep_ref.shape[0], keep_ref.shape[1]
    for at, grad in ((0, grad_k), (HD, grad_v)):
        for piece in range(pieces):
            even = grad[2 * piece * size : (2 * piece + 1) * size]
            odd = grad[(2 * piece + 1) * size : (2 * piece + 2) * size]
            y, x = divmod(piece, pieces // 2)
            x_offset = lax.rem(x + pieces // 2 - place_ref[4], pieces // 2)
            slot = 2 * x_offset + lax.rem(place_ref[3] + y, 2)
            keep_ref[slot, :, at : at + HD] = jnp.where(even_core, even, odd)
            send_ref[slot, :, at : at + HD] = jnp.where(even_core, odd, even)


def term_part(order, place, factors, queries, grad_out, e, es, at, bt, pieces):
    rows, width = queries.shape
    image_rows, wide = e.shape
    heads = factors.shape[1]
    pairs = heads // 2
    groups = heads // 8
    per_group = width // groups
    size = image_rows // (2 * pieces)
    order = [o % (pairs // 2) for o in order]
    offsets = jnp.array(order + order[-2:], jnp.int32)

    def spec(i, slot):
        def index(g, offset, place):
            return 0, pair_at(place, offset[2 * g + i], slot, pairs)

        return pl.BlockSpec((HD, 2 * rows), index)

    four = [spec(i, slot) for i in range(2) for slot in range(2)]
    half = jax.ShapeDtypeStruct((pieces, size, groups * 2 * HD), F32)
    half_spec = pl.BlockSpec((pieces, size, 2 * HD), lambda g, *_: (0, 0, g))
    grid_spec = pltpu.PrefetchScalarGridSpec(
        num_scalar_prefetch=2,
        grid=(groups,),
        in_specs=[
            pl.BlockSpec((2, heads, rows), lambda g, *_: (0, 0, 0)),
            pl.BlockSpec((2, heads // groups, rows), lambda g, *_: (0, g, 0)),
            pl.BlockSpec((rows, per_group), lambda g, *_: (0, g)),
            pl.BlockSpec((rows, per_group), lambda g, *_: (0, g)),
            pl.BlockSpec((image_rows, wide // groups), lambda g, *_: (0, g)),
            pl.BlockSpec((image_rows, wide // groups), lambda g, *_: (0, g)),
            *four,
            *four,
        ],
        out_specs=[pl.BlockSpec((2, 2, rows, 2 * HD), lambda g, *_: (g, 0, 0, 0)), half_spec, half_spec],
        scratch_shapes=[pltpu.VMEM((2, heads, rows), F32)],
    )
    return pl.pallas_call(
        term_kernel,
        grid_spec=grid_spec,
        out_shape=[jax.ShapeDtypeStruct((2 * groups, 2, rows, 2 * HD), F32), half, half],
        compiler_params=pltpu.CompilerParams(vmem_limit_bytes=TERM_LIMIT),
        cost_estimate=pl.CostEstimate(
            flops=6 * width * rows * image_rows, bytes_accessed=20 * 2**20, transcendentals=0
        ),
        name="query_and_image_terms",
    )(offsets, place, factors, factors, queries, grad_out, e, es, *[at] * 4, *[bt] * 4)


def on_device(queries, keys, values, grad_out, keep_blocks):
    image_size = lax.axis_size("image")
    text_size = lax.axis_size("text")
    y_size = 2
    z_size = image_size // y_size
    pieces = text_size // 2
    groups = keys.shape[1] // HD
    swap_far = [(t, (t + pieces) % text_size) for t in range(text_size)]
    swap_core = [(t, t ^ 1) for t in range(text_size)]
    image_index = lax.axis_index("image").astype(jnp.int32)
    text_index = lax.axis_index("text").astype(jnp.int32)
    x_size = pieces // 2
    place = jnp.stack(
        [
            image_index // z_size,
            image_index % z_size,
            text_index % 2,
            text_index // pieces,
            text_index // 2 % x_size,
        ]
    )

    def turn_x(by):
        return [
            (y * pieces + 2 * x + c, y * pieces + (2 * x + 2 * by) % pieces + c)
            for y in range(2)
            for x in range(x_size)
            for c in range(2)
        ]

    def turn(by, across=0):
        return [
            (y * z_size + z, (y + across) % y_size * z_size + (z + by) % z_size)
            for y in range(y_size)
            for z in range(z_size)
        ]

    e, own, maxima = local_part(keep_blocks, queries, grad_out, keys, values, image_size)
    stats = lax.all_to_all(own, "image", 0, 0, tiled=True)
    es, at, bt = product_part(own, grad_out, keys, values, e)

    first_right, first_left, factors = merge_part(place, stats, own, maxima, at, bt)
    right = lax.ppermute(first_right, "image", turn(1))
    left = lax.ppermute(first_left, "image", turn(-1))
    order = piece_offsets(z_size)[2:]
    terms, keep, send = term_part(
        order, place, factors, queries, grad_out, e, es, at, bt, pieces
    )
    terms, keep, send, right, left = lax.optimization_barrier((terms, keep, send, right, left))
    term = {offset: terms[i] for i, offset in enumerate(order)}
    received = lax.ppermute(send, "text", swap_core)
    right = lax.ppermute(right + term[3], "image", turn(1))
    left = lax.ppermute(left + term[-2], "image", turn(-1))
    image_terms = keep + received
    part = [image_terms[2 * by : 2 * by + 2] for by in range(x_size)]
    x_right = lax.ppermute(part[2][0], "text", turn_x(1))
    x_left = lax.ppermute(part[2][1], "text", turn_x(-1))
    right, left, x_right, x_left = lax.optimization_barrier((right, left, x_right, x_left))
    right = lax.ppermute(right + term[2], "image", turn(1))
    left = lax.ppermute(left + term[-1], "image", turn(-1))
    x_right = lax.ppermute(jnp.stack([part[1][0] + x_right, part[1][1]]), "text", turn_x(1))
    x_left = lax.ppermute(jnp.stack([part[3][0], part[3][1] + x_left]), "text", turn_x(-1))
    right, left = lax.optimization_barrier((right, left))
    x_sum = part[0] + x_right + x_left
    image_sum = x_sum[0] + lax.ppermute(x_sum[1], "text", swap_far)
    over = right + term[1]
    here = left + term[0]
    query_sum = (
        here[0]
        + lax.ppermute(over[0], "image", turn(1))
        + lax.ppermute(over[1], "image", turn(1, 1))
        + lax.ppermute(here[1], "image", turn(0, 1))
    )
    grad_queries = query_sum.astype(BF16)
    grad_keys = jnp.concatenate([head(image_sum, 2 * g) for g in range(groups)], axis=1).astype(BF16)
    grad_values = jnp.concatenate([head(image_sum, 2 * g + 1) for g in range(groups)], axis=1).astype(BF16)
    return (grad_queries, grad_keys, grad_values)


def solution(mesh):
    return jax.shard_map(
        on_device,
        mesh=mesh,
        in_specs=(
            P("text", None),
            P("image", None),
            P("image", None),
            P("text", None),
            P("text", "image"),
        ),
        out_specs=(P("text", "image"), P(("image", "text"), None), P(("image", "text"), None)),
        check_vma=False,
    )
```
